32 devices in a mesh: parts: 2 (over y), gx: 4 (over z), gy: 2 (over x), gz: 2 (over core).
Axes of the slice: x: 2, y: 2, z: 4, core: 2. Of those that a mesh axis runs over, the one named last changes fastest.
Arguments:
- atom_types: int32 [131072], P(('parts', 'gx', 'gy', 'gz')), parts along dimension 0, may hold values from 0 to 3
- potential: float32 [131072], P(('parts', 'gx', 'gy', 'gz')), parts along dimension 0, may hold values from -2 to 2
- guess: float32 [2, 131072], P(None, ('parts', 'gx', 'gy', 'gz')), parts along dimension 1, may hold values from -3 to 3
- type_electroneg: float32 [4], replicated, may hold values from 3 to 7
- type_hardness: float32 [4], replicated, may hold values from 1 to 8
- local_tiles: bfloat16 [2048, 128, 128], P(('parts', 'gx', 'gy', 'gz')), parts along dimension 0, may hold values from -0.00083984375 to 0.00083984375
- local_pairs: int32 [2, 2048], P(None, ('parts', 'gx', 'gy', 'gz')), parts along dimension 1, may hold values from 0 to 31, as said below
- local_count: int32 [32], P(('parts', 'gx', 'gy', 'gz')), parts along dimension 0, may hold values from 32 to 64
- ghost_tiles: bfloat16 [2, 1024, 128, 128], P(None, ('parts', 'gx', 'gy', 'gz')), parts along dimension 1, may hold values from -0.00083984375 to 0.00083984375
- ghost_blocks: int32 [2, 1024], P(None, ('parts', 'gx', 'gy', 'gz')), parts along dimension 1, may hold values from 0 to 31, as said below
- send_rows: int32 [2, 131072], P(None, ('parts', 'gx', 'gy', 'gz')), parts along dimension 1, may hold values from 0 to 4095, as said below
Outputs:
- solution: float32 [2, 131072], P(None, ('parts', 'gx', 'gy', 'gz')), parts along dimension 1
The draws below stay inside these ranges and needn't reach their ends.
There are 2 independent parts, one for each index of `parts`. The reference program is written for one: setup_inputs(seed, part) draws one part's arguments, and reference() takes and returns one part's arrays. A program takes and returns all parts, laid end to end along the dimension named above; an argument that names none is the same for every part. Nothing has to cross between parts.
Inputs may be any that keep to these rules, and one draw needn't show every extreme that they name: In each brick's 64 slots, local_pairs[0] names every block 0 to 31 exactly 2 times, and so does local_pairs[1]. `ghost_blocks`: for each direction and brick, the 32 entries are a permutation of the blocks. `send_rows`: for each direction and brick, the 4096 entries are a permutation of the brick's local atom indices; each aligned block of 128 entries starting at a multiple of 128 holds all atoms of one block of the brick.
All inputs are finite; a program needn't handle non-finite values.
Results may differ from the reference program's by a relative error of at most 0.0003.
Values may be sent and summed in bfloat16 or wider, within the bound.
A program may use at most 64 MiB of HBM per device.

```python
import math
import jax
import jax.numpy as jnp
import numpy as np
from jax import lax

TILE = 128
BLOCKS = 32
ROUNDS = 2
NTYPES = 4
ITERS = 3
ATOM_DEV = 4096
LOCAL_TILES = 64
BRICKS = 16
ATOMS = 65536
N_GX = 4
N_GY = 2
N_GZ = 2


def tile_entries(key, tile_dims):
    ceiling = 0.85 / (TILE * (2 * ROUNDS + 4))
    low_end = 0.5
    positive = 0.75
    magnitude = jax.random.uniform(key, tile_dims, jnp.float32, low_end, 1.0)
    signs = jnp.where(jax.random.bernoulli(jax.random.fold_in(key, 1), positive, tile_dims), 1.0, -1.0)
    entries = ceiling * magnitude * signs
    return entries.astype(jnp.bfloat16)


def shuffled_rows(key, count, length):
    key_list = jax.random.split(key, count)
    return jax.vmap(lambda subkey: jax.random.permutation(subkey, length))(key_list).astype(jnp.int32)


def draw_local_tiles(key, part):
    key = jax.random.fold_in(key, 11)
    return tile_entries(key, (BRICKS * LOCAL_TILES, TILE, TILE))


def draw_ghost_tiles(key, part):
    key = jax.random.fold_in(key, 13)
    return tile_entries(key, (2, BRICKS * BLOCKS, TILE, TILE))


def draw_local_pairs(key, part):
    key = jax.random.fold_in(key, 17)
    shuffled = shuffled_rows(key, 2 * BRICKS * ROUNDS, BLOCKS)
    return shuffled.reshape(2, BRICKS * LOCAL_TILES)


def draw_ghost_blocks(key, part):
    key = jax.random.fold_in(key, 19)
    shuffled = shuffled_rows(key, 2 * BRICKS, BLOCKS)
    return shuffled.reshape(2, BRICKS * BLOCKS)


def draw_send_rows(key, part):
    key = jax.random.fold_in(key, 23)
    block_order = shuffled_rows(key, 2 * BRICKS, BLOCKS)
    within = shuffled_rows(jax.random.fold_in(key, 1), 2 * BRICKS * BLOCKS, TILE).reshape(2 * BRICKS, BLOCKS, TILE)
    combined = block_order[:, :, None] * TILE + within
    return combined.astype(jnp.int32).reshape(2, BRICKS * ATOM_DEV)


def touch_ends(drawn, own_key, least, high):
    extent = drawn.shape
    index_at = [jax.random.randint(jax.random.fold_in(own_key, axis), (), 0, extent[axis]) for axis in range(len(extent))]
    drawn = drawn.at[tuple(index_at)].set(least)
    longest = extent.index(max(extent))
    index_at[longest] = (index_at[longest] + 1) % extent[longest]
    return drawn.at[tuple(index_at)].set(high)


def levels(own_key, shape, cuts, low, largest):
    def one(dim, blocks):
        steps = jax.random.uniform(jax.random.fold_in(jax.random.fold_in(own_key, 6), dim), (blocks,), jnp.float32, low / len(cuts), largest / len(cuts))
        return jnp.repeat(jnp.exp(steps), shape[dim] // blocks).reshape((-1,) + (1,) * (len(shape) - dim - 1))

    level = one(*cuts[0])
    for cut in cuts[1:]:
        level = level * one(*cut)
    return level


def gaussian(stream_key, dims, width, limit, shards=(), kind=jnp.bfloat16):
    values = width * jax.random.normal(stream_key, dims, jnp.float32)
    if shards:
        values = values * levels(stream_key, dims, shards, -0.22, 0.18)
    return jnp.clip(values, -limit, limit).astype(kind)


def setup_inputs(seed: int = 0, part: int = 0) -> dict:
    streams_of = jax.random.split(jax.random.key(seed), 12)
    part_keys = jax.random.split(jax.random.fold_in(streams_of[11], part), 12)
    return {
        "atom_types": touch_ends(jax.random.randint(part_keys[0], (ATOMS,), 0, NTYPES), jax.random.fold_in(part_keys[0], 1), 0, NTYPES - 1).astype(jnp.int32),
        "potential": jnp.clip(jax.random.uniform(part_keys[1], (ATOMS,), jnp.float32, -2.0, 2.0) * levels(part_keys[1], (ATOMS,), ((0, 16),), -0.4, 0.0), -2.0, 2.0),
        "guess": gaussian(part_keys[2], (2, ATOMS), 0.5, 3.0, ((1, 16),), jnp.float32),
        "type_electroneg": jnp.clip(jax.random.uniform(streams_of[3], (NTYPES,), jnp.float32, 3.0, 7.0), 3.0, 7.0),
        "type_hardness": jnp.clip(jnp.exp(jax.random.uniform(streams_of[4], (NTYPES,), jnp.float32, math.log(1.0), math.log(8.0))), 1.0, 8.0),
        "local_tiles": draw_local_tiles(jax.random.fold_in(jax.random.fold_in(streams_of[11], part), 71), part),
        "local_pairs": draw_local_pairs(jax.random.fold_in(jax.random.fold_in(streams_of[11], part), 71), part),
        "local_count": touch_ends(jax.random.randint(part_keys[7], (BRICKS,), LOCAL_TILES // 2, LOCAL_TILES + 1), jax.random.fold_in(part_keys[7], 1), LOCAL_TILES // 2, LOCAL_TILES).astype(jnp.int32),
        "ghost_tiles": draw_ghost_tiles(jax.random.fold_in(jax.random.fold_in(streams_of[11], part), 71), part),
        "ghost_blocks": draw_ghost_blocks(jax.random.fold_in(jax.random.fold_in(streams_of[11], part), 71), part),
        "send_rows": draw_send_rows(jax.random.fold_in(jax.random.fold_in(streams_of[11], part), 71), part),
    }


def lookup(atom_ids, table):
    type_codes = jnp.arange(table.shape[0], dtype=jnp.int32)
    return jnp.sum(jnp.where(atom_ids[None, :] == type_codes[:, None], table[:, None], jnp.float32(0.0)), axis=0)


def pick_blocks(vector, chosen):
    shaped = vector.reshape(vector.shape[0], -1, TILE)
    return jnp.take(shaped, chosen, axis=1)


def spread(values, chosen, blocks):
    onehot = (chosen[:, None] == jnp.arange(blocks, dtype=jnp.int32)[None, :]).astype(jnp.float32)
    summed = jnp.einsum("kb,skt->sbt", onehot, values, precision=lax.Precision.HIGHEST)
    return summed.reshape(values.shape[0], blocks * TILE)


def forward(tile_set, pieces):
    return jnp.einsum("krc,skc->skr", tile_set.astype(jnp.float32), pieces, precision=lax.Precision.HIGHEST)


def transposed(tile_set, pieces):
    return jnp.einsum("krc,skr->skc", tile_set.astype(jnp.float32), pieces, precision=lax.Precision.HIGHEST)


def operate(vector, hardness, tiles_local, rows_local, cols_local, living, tiles_ghost, blocks_ghost, send_all, neighbours):
    blocks = vector.shape[2] // TILE

    def local_brick(inputs):
        brick_vec, tile_set, row_ids, col_ids, alive_mask = inputs
        onward = forward(tile_set, pick_blocks(brick_vec, col_ids)) * alive_mask[None, :, None]
        behind = transposed(tile_set, pick_blocks(brick_vec, row_ids)) * alive_mask[None, :, None]
        return spread(onward, row_ids, blocks) + spread(behind, col_ids, blocks)

    result = hardness[:, None, :] * vector + lax.map(local_brick, (vector, tiles_local, rows_local, cols_local, living))
    for side_index in range(2):
        following = neighbours[side_index]
        preceding = np.argsort(following)
        send_ids = send_all[side_index]
        exported = jax.vmap(lambda brick_vec, indices: brick_vec[:, indices])(vector, send_ids)
        ghosts = exported[following]

        def ghost_brick(inputs):
            brick_vec, ghost_rows, tile_set, chosen = inputs
            onward = forward(tile_set, ghost_rows.reshape(2, -1, TILE))
            behind = transposed(tile_set, pick_blocks(brick_vec, chosen)).reshape(2, -1)
            return spread(onward, chosen, blocks), behind

        nearby, behind = lax.map(ghost_brick, (vector, ghosts, tiles_ghost[side_index], blocks_ghost[side_index]))
        returned = behind[preceding]
        owner_terms = jax.vmap(lambda indices, values: jnp.zeros(values.shape, jnp.float32).at[:, indices].add(values))(send_ids, returned)
        result = result + nearby + owner_terms
    return result


def reference(atom_types, potential, guess, type_electroneg, type_hardness, local_tiles, local_pairs, local_count, ghost_tiles, ghost_blocks, send_rows):
    bricks = N_GX * N_GY * N_GZ
    across = N_GY * N_GZ
    numbers = np.arange(bricks)
    neighbours = (((numbers // across + 1) % N_GX) * across + numbers % across,
                  (numbers // across) * across + (numbers % across + 1) % across)
    electro = lookup(atom_types, type_electroneg).reshape(bricks, ATOM_DEV)
    hardness = lookup(atom_types, type_hardness).reshape(bricks, ATOM_DEV)
    target = jnp.stack([-(electro + potential.reshape(bricks, ATOM_DEV)), -jnp.ones((bricks, ATOM_DEV), jnp.float32)], axis=1)
    tiles_local = local_tiles.reshape(bricks, LOCAL_TILES, TILE, TILE)
    pairs_local = local_pairs.reshape(2, bricks, LOCAL_TILES)
    living = (jnp.arange(LOCAL_TILES, dtype=jnp.int32)[None, :] < local_count[:, None]).astype(jnp.float32)
    tiles_ghost = ghost_tiles.reshape(2, bricks, BLOCKS, TILE, TILE)
    blocks_ghost = ghost_blocks.reshape(2, bricks, BLOCKS)
    send_all = send_rows.reshape(2, bricks, ATOM_DEV)

    def apply_operator(vector):
        return operate(vector, hardness, tiles_local, pairs_local[0], pairs_local[1], living, tiles_ghost, blocks_ghost, send_all, neighbours)

    iterate = guess.reshape(2, bricks, ATOM_DEV).transpose(1, 0, 2)
    residual = target - apply_operator(iterate)
    direction = residual
    norm_now = jnp.sum(residual * residual, axis=(0, 2))
    for sweep_index in range(ITERS):
        product_vec = apply_operator(direction)
        step_size = norm_now / jnp.sum(direction * product_vec, axis=(0, 2))
        iterate = iterate + step_size[None, :, None] * direction
        if sweep_index + 1 < ITERS:
            residual = residual - step_size[None, :, None] * product_vec
            norm_next = jnp.sum(residual * residual, axis=(0, 2))
            direction = residual + (norm_next / norm_now)[None, :, None] * direction
            norm_now = norm_next
    return iterate.transpose(1, 0, 2).reshape(2, bricks * ATOM_DEV)
```

```python
import functools

import jax
import jax.numpy as jnp
from jax import lax
from jax.experimental import pallas as pl
from jax.experimental.pallas import tpu as pltpu
from jax.sharding import PartitionSpec as P

TILE = 128
ITERS = 3
DIRECT = 16
MESH = pl.DeviceIdType.MESH
F32 = jnp.float32
I32 = jnp.int32
NT = (((1,), (1,)), ((), ()))
NN = (((1,), (0,)), ((), ()))


def dot(lhs, rhs, dims):
    return lax.dot_general(lhs, rhs, dims, preferred_element_type=F32)


def places(sizes):
    n_gx, n_gy, n_gz = sizes
    across = n_gy * n_gz
    u = lax.axis_index("gx")
    v = lax.axis_index("gy") * n_gz + lax.axis_index("gz")

    def brick(u_at, v_at):
        return {"gx": u_at, "gy": v_at // n_gz, "gz": lax.rem(v_at, n_gz)}

    def shift(at, by, size):
        return lax.rem(at + by, size)

    ahead = (brick(shift(u, 1, n_gx), v), brick(u, shift(v, 1, across)))
    back = (brick(shift(u, n_gx - 1, n_gx), v), brick(u, shift(v, across - 1, across)))
    whole = n_gx * across
    if whole <= DIRECT:
        me = u * across + v

        def peer(step):
            at = lax.rem(me + step, whole)
            return brick(at // across, lax.rem(at, across))

        stages = [(whole, me, peer)]
    else:
        stages = [
            (n_gx, u, lambda step: brick(shift(u, step, n_gx), v)),
            (across, v, lambda step: brick(u, shift(v, step, across))),
        ]
    return ahead, back, stages


def kernel(
    sizes,
    types_ref,
    potential_ref,
    guess_ref,
    electro_ref,
    hard_ref,
    local_hbm,
    pairs_ref,
    count_ref,
    ghost_hbm,
    gblocks_ref,
    gblocks_s,
    send_ref,
    out_ref,
    lt,
    gt,
    gp,
    rows,
    rows_in,
    table_v,
    table_s,
    own_v,
    own_s,
    next_v,
    next_s,
    vec,
    vec_in,
    part,
    part_in,
    lh,
    gl,
    hd,
    xs,
    rs,
    ps,
    red,
    load_sem,
    rows_sem,
    vec_sem,
    part_sem,
    red_sem,
):
    blocks = types_ref.shape[0]
    ahead, back, stages = places(sizes)

    barrier = pltpu.get_barrier_semaphore()
    greeted = 0
    for size, _, peer in stages:
        greeted += size - 1
        for step in range(1, size):
            pl.semaphore_signal(barrier, inc=1, device_id=peer(step), device_id_type=MESH)

    load_local = pltpu.make_async_copy(local_hbm, lt, load_sem.at[0])
    load_local.start()
    load_ghost = pltpu.make_async_copy(ghost_hbm, gt, load_sem.at[1])
    load_ghost.start()

    for b in range(blocks):
        cut = slice(b * TILE, (b + 1) * TILE)
        piece = send_ref[:, cut]
        rows[0, b : b + 1, :] = piece[0:1]
        rows[1, b : b + 1, :] = piece[1:2]
        begin = guess_ref[:, cut]
        vec[0, b] = begin
        xs[b] = begin

    slots = pairs_ref.shape[1]
    slot = lax.broadcasted_iota(I32, (blocks, slots), 1)
    block = lax.broadcasted_iota(I32, (blocks, slots), 0)
    live = slot < count_ref[0]
    pair_row = jnp.broadcast_to(pairs_ref[0:1, :], (blocks, slots))
    pair_col = jnp.broadcast_to(pairs_ref[1:2, :], (blocks, slots))
    columns = []
    partners = []
    for mine, other in ((pair_row, pair_col), (pair_col, pair_row)):
        hit = mine == block
        first = jnp.min(jnp.where(hit, slot, slots - 1), axis=1, keepdims=True)
        last = jnp.max(jnp.where(hit, slot, 0), axis=1, keepdims=True)
        for found in (first, last):
            columns.append(found)
            value = jnp.where(live, other, blocks)
            partners.append(
                jnp.max(jnp.where(slot == found, value, 0), axis=1, keepdims=True)
            )
    columns = columns + partners
    slot_g = lax.broadcasted_iota(I32, (blocks, blocks), 1)
    block_g = lax.broadcasted_iota(I32, (blocks, blocks), 0)
    for d in range(2):
        named = jnp.broadcast_to(gblocks_ref[d : d + 1, :], (blocks, blocks))
        columns.append(jnp.max(jnp.where(named == block_g, slot_g, 0), axis=1, keepdims=True))
    lane = lax.broadcasted_iota(I32, (blocks, TILE), 1)
    table = jnp.zeros((blocks, TILE), I32)
    for q, column in enumerate(columns):
        table = jnp.where(lane == q, column, table)
    table_v[...] = table
    load_table = pltpu.make_async_copy(table_v, table_s, load_sem.at[2])
    load_table.start()
    own_v[...] = jnp.zeros(own_v.shape, I32)
    slot_k = lax.broadcasted_iota(I32, (blocks, TILE), 0)
    for d in range(2):
        at = jnp.broadcast_to(rows[d][:, 0:1] // TILE, (blocks, TILE))
        own_v[d : d + 1, :] = jnp.max(
            jnp.where(at == lane, slot_k, 0), axis=0, keepdims=True
        )
    load_own = pltpu.make_async_copy(own_v, own_s, load_sem.at[3])
    load_own.start()

    pl.semaphore_wait(barrier, greeted)

    rows_copy = []
    for d in range(2):
        copy = pltpu.make_async_remote_copy(
            src_ref=rows.at[d],
            dst_ref=rows_in.at[d],
            send_sem=rows_sem.at[0, d],
            recv_sem=rows_sem.at[1, d],
            device_id=back[d],
            device_id_type=MESH,
        )
        copy.start()
        rows_copy.append(copy)

    def send(buffer, landing, sems, apply, d, target):
        copy = pltpu.make_async_remote_copy(
            src_ref=buffer,
            dst_ref=landing,
            send_sem=sems.at[0, apply, d],
            recv_sem=sems.at[1, apply, d],
            device_id=target,
            device_id_type=MESH,
        )
        copy.start()
        return copy

    types = types_ref[...]
    hard = jnp.zeros(types.shape, F32)
    electro = jnp.zeros(types.shape, F32)
    for code in range(hard_ref.shape[0]):
        hard = jnp.where(types == code, hard_ref[code], hard)
        electro = jnp.where(types == code, electro_ref[code], electro)
    wanted = -(electro + potential_ref[...])
    system = lax.broadcasted_iota(I32, (2, TILE), 0)
    for b in range(blocks):
        hd[b] = jnp.broadcast_to(hard[b : b + 1], (2, TILE))
        rs[b] = jnp.where(system == 0, jnp.broadcast_to(wanted[b : b + 1], (2, TILE)), -1.0)

    lh[blocks] = jnp.zeros((8, TILE), F32)
    top = lax.broadcasted_iota(I32, (8, TILE), 0) < 4

    def split(vector):
        upper = vector.astype(jnp.bfloat16).astype(F32)
        return jnp.concatenate([upper, vector - upper] * 2, axis=1)

    def join(one, two):
        return jnp.where(top, one, two).astype(jnp.bfloat16)

    def parts_of(both):
        one = both[0:2, :TILE] + both[2:4, :TILE]
        two = both[4:6, TILE:] + both[6:8, TILE:]
        return one, two

    def square(a, b, c, d):
        return jnp.concatenate(
            [jnp.concatenate([a, b], axis=1), jnp.concatenate([c, d], axis=1)], axis=0
        )

    def looped(steps, unroll, body):
        def run(outer, carry):
            for inner in range(unroll):
                body(outer * unroll + inner)
            return carry

        lax.fori_loop(0, steps // unroll, run, 0)

    def local_part(apply):
        def body(pair):
            one = pair * 2
            two = one + 1
            s = [(table_s[one, q], table_s[two, q]) for q in range(8)]
            left = jnp.concatenate(
                [join(lh[s[4][0]], lh[s[4][1]]), join(lh[s[5][0]], lh[s[5][1]])], axis=1
            )
            onward = dot(
                left, square(lt[s[0][0]], lt[s[1][0]], lt[s[0][1]], lt[s[1][1]]), NT
            )
            left = jnp.concatenate(
                [join(lh[s[6][0]], lh[s[6][1]]), join(lh[s[7][0]], lh[s[7][1]])], axis=1
            )
            behind = dot(
                left, square(lt[s[2][0]], lt[s[2][1]], lt[s[3][0]], lt[s[3][1]]), NN
            )
            sum_one, sum_two = parts_of(onward + behind)
            ps[one] = hd[one] * vec[apply, one] + sum_one
            ps[two] = hd[two] * vec[apply, two] + sum_two

        looped(blocks // 2, 4, body)

    def partials(apply):
        def body(k):
            left = join(lh[gblocks_s[0, k]], lh[gblocks_s[1, k]])
            both = dot(left, jnp.concatenate([gp[0, k], gp[1, k]], axis=1), NN)
            zero, first = parts_of(both)
            part[apply, 0, k] = zero
            part[apply, 1, k] = first

        looped(blocks, 8, body)

    def ghost_part():
        def body(pair):
            one = pair * 2
            two = one + 1
            k0 = (table_s[one, 8], table_s[two, 8])
            k1 = (table_s[one, 9], table_s[two, 9])
            left = jnp.concatenate(
                [
                    join(gl[0, next_s[k0[0], 0]], gl[0, next_s[k0[1], 0]]),
                    join(gl[1, next_s[k1[0], 1]], gl[1, next_s[k1[1], 1]]),
                ],
                axis=1,
            )
            sum_one, sum_two = parts_of(
                dot(left, square(gp[0, k0[0]], gp[1, k1[0]], gp[0, k0[1]], gp[1, k1[1]]), NT)
            )
            ps[one] = ps[one] + sum_one
            ps[two] = ps[two] + sum_two

        looped(blocks // 2, 4, body)

    def returned(apply):
        def body(b):
            ps[b] = ps[b] + (part_in[apply][0][own_s[0, b]] + part_in[apply][1][own_s[1, b]])

        looped(blocks, 8, body)

    def reorder():
        within_at = lax.broadcasted_iota(I32, (TILE, TILE), 0)

        for d in range(2):

            def body(k):
                within = rows_in[d, pl.ds(k, 1), :]
                within = within - (within // TILE) * TILE
                chosen = jnp.where(within == within_at, 1.0, 0.0).astype(jnp.bfloat16)
                gp[d, k] = dot(gt[d, k], chosen, NT).astype(jnp.bfloat16)

            looped(blocks, 4, body)

    pending = []
    for apply in range(ITERS + 1):
        incoming = []
        for d in range(2):
            incoming.append(
                send(vec.at[apply], vec_in.at[apply, d], vec_sem, apply, d, back[d])
            )
        lh[0:blocks] = split(vec[apply])
        if apply == 0:
            load_local.wait()
            load_table.wait()
            local_part(apply)
            load_ghost.wait()
            for copy in rows_copy:
                copy.wait()
            columns = jnp.zeros((blocks, TILE), I32)
            for d in range(2):
                columns = jnp.where(lane == d, rows_in[d][:, 0:1] // TILE, columns)
            next_v[...] = columns
            load_next = pltpu.make_async_copy(next_v, next_s, load_sem.at[4])
            load_next.start()
            reorder()
            load_next.wait()
            load_own.wait()
        partials(apply)
        back_copies = []
        for d in range(2):
            back_copies.append(
                send(part.at[apply, d], part_in[apply][d], part_sem, apply, d, ahead[d])
            )
        if apply > 0:
            local_part(apply)
        for d in range(2):
            incoming[d].wait()
            gl[d] = split(vec_in[apply, d])
        ghost_part()
        for copy in back_copies:
            copy.wait()
        returned(apply)
        product = ps[...]
        if apply == 0:
            residual = rs[...] - product
            rs[...] = residual
            vec[1] = residual
            continue

        residual = rs[...]
        direction = vec[apply]
        sums = jnp.concatenate(
            [
                jnp.sum(a * b, axis=0)
                for a, b in (
                    (residual, residual),
                    (direction, product),
                    (residual, product),
                    (product, product),
                )
            ],
            axis=0,
        )
        offset = 0
        sem_at = 0
        for size, me, peer in stages:
            mine = offset + me
            red[apply - 1, mine] = sums
            copies = []
            for step in range(1, size):
                copy = pltpu.make_async_remote_copy(
                    src_ref=red.at[apply - 1, mine],
                    dst_ref=red.at[apply - 1, mine],
                    send_sem=red_sem.at[0, apply - 1, sem_at],
                    recv_sem=red_sem.at[1, apply - 1, sem_at],
                    device_id=peer(step),
                    device_id_type=MESH,
                )
                copy.start()
                copies.append(copy)
                sem_at += 1
            for copy in copies:
                copy.wait()
            sums = jnp.sum(red[apply - 1, offset : offset + size], axis=0)
            offset += size
        totals = jnp.broadcast_to(jnp.sum(sums, axis=1, keepdims=True), (8, TILE))
        norm_now = totals[0:2]
        step_size = norm_now / totals[2:4]
        found = xs[...] + step_size[None] * direction
        if apply == ITERS:
            xs[...] = found
        else:
            xs[...] = found
            ratio = jnp.maximum(
                (norm_now + step_size * (step_size * totals[6:8] - 2.0 * totals[4:6])) / norm_now,
                0.0,
            )
            residual = residual - step_size[None] * product
            rs[...] = residual
            vec[apply + 1] = residual + ratio[None] * direction

    for b in range(blocks):
        out_ref[:, b * TILE : (b + 1) * TILE] = xs[b]


def shards(
    sizes,
    atom_types,
    potential,
    guess,
    type_electroneg,
    type_hardness,
    local_tiles,
    local_pairs,
    local_count,
    ghost_tiles,
    ghost_blocks,
    send_rows,
):
    blocks = guess.shape[1] // TILE
    slots = local_tiles.shape[0]
    n_gx, n_gy, n_gz = sizes
    if n_gx * n_gy * n_gz <= DIRECT:
        places_held, peers = n_gx * n_gy * n_gz, n_gx * n_gy * n_gz - 1
    else:
        places_held, peers = n_gx + n_gy * n_gz, n_gx + n_gy * n_gz - 2
    vmem = pl.BlockSpec(memory_space=pltpu.VMEM)
    smem = pl.BlockSpec(memory_space=pltpu.SMEM)
    hbm = pl.BlockSpec(memory_space=pl.ANY)
    applies = ITERS + 1
    vector = (blocks, 2, TILE)
    dma = pltpu.SemaphoreType.DMA
    call = pl.pallas_call(
        functools.partial(kernel, sizes),
        out_shape=jax.ShapeDtypeStruct(guess.shape, F32),
        in_specs=[vmem, vmem, vmem, smem, smem, hbm, vmem, smem, hbm, vmem, smem, vmem],
        out_specs=vmem,
        scratch_shapes=[
            pltpu.VMEM((slots, TILE, TILE), jnp.bfloat16),
            pltpu.VMEM((2, blocks, TILE, TILE), jnp.bfloat16),
            pltpu.VMEM((2, blocks, TILE, TILE), jnp.bfloat16),
            pltpu.VMEM((2, blocks, TILE), I32),
            pltpu.VMEM((2, blocks, TILE), I32),
            pltpu.VMEM((blocks, TILE), I32),
            pltpu.SMEM((blocks, TILE), I32),
            pltpu.VMEM((8, TILE), I32),
            pltpu.SMEM((8, TILE), I32),
            pltpu.VMEM((blocks, TILE), I32),
            pltpu.SMEM((blocks, TILE), I32),
            pltpu.VMEM((applies,) + vector, F32),
            pltpu.VMEM((applies, 2) + vector, F32),
            pltpu.VMEM((applies, 2) + vector, F32),
            [[pltpu.VMEM(vector, F32)] * 2 for _ in range(applies)],
            pltpu.VMEM((blocks + 1, 8, TILE), F32),
            pltpu.VMEM((2, blocks, 8, TILE), F32),
            pltpu.VMEM(vector, F32),
            pltpu.VMEM(vector, F32),
            pltpu.VMEM(vector, F32),
            pltpu.VMEM(vector, F32),
            pltpu.VMEM((ITERS, places_held, 8, TILE), F32),
            dma((5,)),
            dma((2, 2)),
            dma((2, applies, 2)),
            dma((2, applies, 2)),
            dma((2, ITERS, peers)),
        ],
        compiler_params=pltpu.CompilerParams(
            collective_id=0, has_side_effects=True, vmem_limit_bytes=40 * 1024 * 1024
        ),
        name="charges",
    )
    return call(
        atom_types.reshape(blocks, TILE),
        potential.reshape(blocks, TILE),
        guess,
        type_electroneg,
        type_hardness,
        local_tiles,
        local_pairs,
        local_count,
        ghost_tiles,
        ghost_blocks,
        ghost_blocks,
        send_rows,
    )


def solution(mesh):
    everywhere = ("parts", "gx", "gy", "gz")
    in_specs = (
        P(everywhere),
        P(everywhere),
        P(None, everywhere),
        P(),
        P(),
        P(everywhere, None, None),
        P(None, everywhere),
        P(everywhere),
        P(None, everywhere, None, None),
        P(None, everywhere),
        P(None, everywhere),
    )
    sizes = tuple(mesh.shape[name] for name in ("gx", "gy", "gz"))
    return jax.shard_map(
        functools.partial(shards, sizes),
        mesh=mesh,
        in_specs=in_specs,
        out_specs=P(None, everywhere),
        check_vma=False,
    )
```

```python
import functools

import jax
import jax.numpy as jnp
from jax import lax
from jax.experimental import pallas as pl
from jax.experimental.pallas import tpu as pltpu
from jax.sharding import PartitionSpec as P

TILE = 128
ITERS = 3
DIRECT = 16
REACH = 0.9
MESH = pl.DeviceIdType.MESH
F32 = jnp.float32
I32 = jnp.int32
NT = (((1,), (1,)), ((), ()))
NN = (((1,), (0,)), ((), ()))


def dot(lhs, rhs, dims):
    return lax.dot_general(lhs, rhs, dims, preferred_element_type=F32)


def places(sizes):
    n_gx, n_gy, n_gz = sizes
    across = n_gy * n_gz
    u = lax.axis_index("gx")
    v = lax.axis_index("gy") * n_gz + lax.axis_index("gz")

    def brick(u_at, v_at):
        return {"gx": u_at, "gy": v_at // n_gz, "gz": lax.rem(v_at, n_gz)}

    def shift(at, by, size):
        return lax.rem(at + by, size)

    ahead = (brick(shift(u, 1, n_gx), v), brick(u, shift(v, 1, across)))
    back = (brick(shift(u, n_gx - 1, n_gx), v), brick(u, shift(v, across - 1, across)))
    whole = n_gx * across
    if whole <= DIRECT:
        me = u * across + v

        def peer(step):
            at = lax.rem(me + step, whole)
            return brick(at // across, lax.rem(at, across))

        stages = [(whole, me, peer)]
    else:
        stages = [
            (n_gx, u, lambda step: brick(shift(u, step, n_gx), v)),
            (across, v, lambda step: brick(u, shift(v, step, across))),
        ]
    return ahead, back, stages


def kernel(
    sizes,
    types_hbm,
    potential_hbm,
    guess_hbm,
    electro_hbm,
    hard_hbm,
    local_hbm,
    pairs_hbm,
    count_hbm,
    ghost_hbm,
    gblocks_hbm,
    send_hbm,
    out_ref,
    types_ref,
    potential_ref,
    guess_ref,
    electro_ref,
    hard_ref,
    pairs_ref,
    count_ref,
    gblocks_ref,
    gblocks_s,
    send_ref,
    small_sem,
    lt,
    gt,
    gp,
    rows,
    rows_in,
    table_v,
    table_s,
    own_v,
    own_s,
    next_v,
    next_s,
    vec,
    vec_in,
    part,
    part_in,
    lh,
    gl,
    hd,
    xs,
    rs,
    ps,
    red,
    load_sem,
    rows_sem,
    vec_sem,
    part_sem,
    red_sem,
):
    blocks = types_hbm.shape[0]
    ahead, back, stages = places(sizes)

    barrier = pltpu.get_barrier_semaphore()
    greeted = 0
    for size, _, peer in stages:
        greeted += size - 1
        for step in range(1, size):
            pl.semaphore_signal(barrier, inc=1, device_id=peer(step), device_id_type=MESH)

    small = []
    for at, (source, target) in enumerate(
        (
            (send_hbm, send_ref),
            (guess_hbm, guess_ref),
            (pairs_hbm, pairs_ref),
            (count_hbm, count_ref),
            (gblocks_hbm, gblocks_ref),
            (gblocks_hbm, gblocks_s),
            (types_hbm, types_ref),
            (potential_hbm, potential_ref),
            (electro_hbm, electro_ref),
            (hard_hbm, hard_ref),
        )
    ):
        copy = pltpu.make_async_copy(source, target, small_sem.at[at])
        copy.start()
        small.append(copy)
    load_local = pltpu.make_async_copy(local_hbm, lt, load_sem.at[0])
    load_local.start()
    load_ghost = pltpu.make_async_copy(ghost_hbm, gt, load_sem.at[1])
    load_ghost.start()

    for copy in small:
        copy.wait()
    for b in range(blocks):
        cut = slice(b * TILE, (b + 1) * TILE)
        piece = send_ref[:, cut]
        rows[0, b : b + 1, :] = piece[0:1]
        rows[1, b : b + 1, :] = piece[1:2]
        begin = guess_ref[:, cut]
        vec[0, b] = begin

    slots = pairs_ref.shape[1]
    slot = lax.broadcasted_iota(I32, (blocks, slots), 1)
    block = lax.broadcasted_iota(I32, (blocks, slots), 0)
    live = slot < count_ref[0]
    pair_row = jnp.broadcast_to(pairs_ref[0:1, :], (blocks, slots))
    pair_col = jnp.broadcast_to(pairs_ref[1:2, :], (blocks, slots))
    columns = []
    partners = []
    for mine, other in ((pair_row, pair_col), (pair_col, pair_row)):
        hit = mine == block
        first = jnp.min(jnp.where(hit, slot, slots - 1), axis=1, keepdims=True)
        last = jnp.max(jnp.where(hit, slot, 0), axis=1, keepdims=True)
        for found in (first, last):
            columns.append(found)
            value = jnp.where(live, other, blocks)
            partners.append(
                jnp.max(jnp.where(slot == found, value, 0), axis=1, keepdims=True)
            )
    columns = columns + partners
    slot_g = lax.broadcasted_iota(I32, (blocks, blocks), 1)
    block_g = lax.broadcasted_iota(I32, (blocks, blocks), 0)
    for d in range(2):
        named = jnp.broadcast_to(gblocks_ref[d : d + 1, :], (blocks, blocks))
        columns.append(jnp.max(jnp.where(named == block_g, slot_g, 0), axis=1, keepdims=True))
    lane = lax.broadcasted_iota(I32, (blocks, TILE), 1)
    table = jnp.zeros((blocks, TILE), I32)
    for q, column in enumerate(columns):
        table = jnp.where(lane == q, column, table)
    table_v[...] = table
    load_table = pltpu.make_async_copy(table_v, table_s, load_sem.at[2])
    load_table.start()
    own_v[...] = jnp.zeros(own_v.shape, I32)
    slot_k = lax.broadcasted_iota(I32, (blocks, TILE), 0)
    for d in range(2):
        at = jnp.broadcast_to(rows[d][:, 0:1] // TILE, (blocks, TILE))
        own_v[d : d + 1, :] = jnp.max(
            jnp.where(at == lane, slot_k, 0), axis=0, keepdims=True
        )
    load_own = pltpu.make_async_copy(own_v, own_s, load_sem.at[3])
    load_own.start()

    pl.semaphore_wait(barrier, greeted)

    rows_copy = []
    for d in range(2):
        copy = pltpu.make_async_remote_copy(
            src_ref=rows.at[d],
            dst_ref=rows_in.at[d],
            send_sem=rows_sem.at[0, d],
            recv_sem=rows_sem.at[1, d],
            device_id=back[d],
            device_id_type=MESH,
        )
        copy.start()
        rows_copy.append(copy)

    def send(buffer, landing, sems, apply, d, target):
        copy = pltpu.make_async_remote_copy(
            src_ref=buffer,
            dst_ref=landing,
            send_sem=sems.at[0, apply, d],
            recv_sem=sems.at[1, apply, d],
            device_id=target,
            device_id_type=MESH,
        )
        copy.start()
        return copy

    types = types_ref[...]
    hard = jnp.zeros(types.shape, F32)
    electro = jnp.zeros(types.shape, F32)
    for code in range(hard_ref.shape[0]):
        hard = jnp.where(types == code, hard_ref[code], hard)
        electro = jnp.where(types == code, electro_ref[code], electro)
    wanted = -(electro + potential_ref[...])
    system = lax.broadcasted_iota(I32, (2, TILE), 0)
    least = jnp.full((2, TILE), hard_ref[0], F32)
    most = least
    for code in range(1, hard_ref.shape[0]):
        least = jnp.minimum(least, hard_ref[code])
        most = jnp.maximum(most, hard_ref[code])
    lowest = least - REACH
    highest = most + REACH
    middle = 0.5 * (least + most)
    scale = 0.5 * (most - least + REACH)
    shrink = 1.0 / scale
    for b in range(blocks):
        hd[b] = jnp.broadcast_to(hard[b : b + 1], (2, TILE))
        rs[b] = jnp.where(system == 0, jnp.broadcast_to(wanted[b : b + 1], (2, TILE)), -1.0)

    lh[blocks] = jnp.zeros((8, TILE), F32)
    top = lax.broadcasted_iota(I32, (8, TILE), 0) < 4

    def split(vector):
        upper = vector.astype(jnp.bfloat16).astype(F32)
        return jnp.concatenate([upper, vector - upper] * 2, axis=1)

    def join(one, two):
        return jnp.where(top, one, two).astype(jnp.bfloat16)

    def parts_of(both):
        one = both[0:2, :TILE] + both[2:4, :TILE]
        two = both[4:6, TILE:] + both[6:8, TILE:]
        return one, two

    def square(a, b, c, d):
        return jnp.concatenate(
            [jnp.concatenate([a, b], axis=1), jnp.concatenate([c, d], axis=1)], axis=0
        )

    def looped(steps, unroll, body):
        def run(outer, carry):
            for inner in range(unroll):
                body(outer * unroll + inner)
            return carry

        lax.fori_loop(0, steps // unroll, run, 0)

    def local_part(apply):
        def body(pair):
            one = pair * 2
            two = one + 1
            s = [(table_s[one, q], table_s[two, q]) for q in range(8)]
            left = jnp.concatenate(
                [join(lh[s[4][0]], lh[s[4][1]]), join(lh[s[5][0]], lh[s[5][1]])], axis=1
            )
            onward = dot(
                left, square(lt[s[0][0]], lt[s[1][0]], lt[s[0][1]], lt[s[1][1]]), NT
            )
            left = jnp.concatenate(
                [join(lh[s[6][0]], lh[s[6][1]]), join(lh[s[7][0]], lh[s[7][1]])], axis=1
            )
            behind = dot(
                left, square(lt[s[2][0]], lt[s[2][1]], lt[s[3][0]], lt[s[3][1]]), NN
            )
            sum_one, sum_two = parts_of(onward + behind)
            ps[one] = hd[one] * vec[apply, one] + sum_one
            ps[two] = hd[two] * vec[apply, two] + sum_two

        looped(blocks // 2, 4, body)

    def partials(apply):
        def body(k):
            left = join(lh[gblocks_s[0, k]], lh[gblocks_s[1, k]])
            both = dot(left, jnp.concatenate([gp[0, k], gp[1, k]], axis=1), NN)
            zero, first = parts_of(both)
            part[apply, 0, k] = zero
            part[apply, 1, k] = first

        looped(blocks, 8, body)

    def ghost_part():
        def body(pair):
            one = pair * 2
            two = one + 1
            k0 = (table_s[one, 8], table_s[two, 8])
            k1 = (table_s[one, 9], table_s[two, 9])
            left = jnp.concatenate(
                [
                    join(gl[0, next_s[k0[0], 0]], gl[0, next_s[k0[1], 0]]),
                    join(gl[1, next_s[k1[0], 1]], gl[1, next_s[k1[1], 1]]),
                ],
                axis=1,
            )
            sum_one, sum_two = parts_of(
                dot(left, square(gp[0, k0[0]], gp[1, k1[0]], gp[0, k0[1]], gp[1, k1[1]]), NT)
            )
            ps[one] = ps[one] + sum_one
            ps[two] = ps[two] + sum_two

        looped(blocks // 2, 4, body)

    def returned(apply):
        def body(b):
            ps[b] = ps[b] + (part_in[apply][0][own_s[0, b]] + part_in[apply][1][own_s[1, b]])

        looped(blocks, 8, body)

    def reorder():
        within_at = lax.broadcasted_iota(I32, (TILE, TILE), 0)

        for d in range(2):

            def body(k):
                within = rows_in[d, pl.ds(k, 1), :]
                within = within - (within // TILE) * TILE
                chosen = jnp.where(within == within_at, 1.0, 0.0).astype(jnp.bfloat16)
                gp[d, k] = dot(gt[d, k], chosen, NT).astype(jnp.bfloat16)

            looped(blocks, 4, body)

    pending = []
    for apply in range(ITERS + 1):
        incoming = []
        for d in range(2):
            incoming.append(
                send(vec.at[apply], vec_in.at[apply, d], vec_sem, apply, d, back[d])
            )
        lh[0:blocks] = split(vec[apply])
        if apply == 0:
            load_local.wait()
            load_table.wait()
            local_part(apply)
            load_ghost.wait()
            for copy in rows_copy:
                copy.wait()
            columns = jnp.zeros((blocks, TILE), I32)
            for d in range(2):
                columns = jnp.where(lane == d, rows_in[d][:, 0:1] // TILE, columns)
            next_v[...] = columns
            load_next = pltpu.make_async_copy(next_v, next_s, load_sem.at[4])
            load_next.start()
            reorder()
            load_next.wait()
            load_own.wait()
        partials(apply)
        back_copies = []
        for d in range(2):
            back_copies.append(
                send(part.at[apply, d], part_in[apply][d], part_sem, apply, d, ahead[d])
            )
        if apply > 0:
            local_part(apply)
        for d in range(2):
            incoming[d].wait()
            gl[d] = split(vec_in[apply, d])
        ghost_part()
        for copy in back_copies:
            copy.wait()
        returned(apply)
        product = ps[...]
        if apply == 0:
            vec[1] = rs[...] - product
        elif apply < ITERS:
            vec[apply + 1] = (product - middle[None] * vec[apply]) * shrink[None]
        else:
            beyond = (product - middle[None] * vec[apply]) * shrink[None]

    basis = [vec[apply] for apply in range(1, ITERS + 1)] + [beyond]
    moments = 2 * ITERS
    dots = [jnp.sum(basis[q // 2] * basis[(q + 1) // 2], axis=0) for q in range(moments)]
    dots += [jnp.zeros((2, TILE), F32)] * (-moments % 4)
    dots = jnp.concatenate(dots, axis=0)
    sums = jnp.sum(dots, axis=1, keepdims=True)
    lanes = lax.broadcasted_iota(I32, dots.shape, 1)
    lines = lax.broadcasted_iota(I32, dots.shape, 0)
    sums = jnp.sum(
        jnp.where(lanes == lines, jnp.broadcast_to(sums, dots.shape), 0.0), axis=0, keepdims=True
    )
    offset = 0
    sem_at = 0
    for size, me, peer in stages:
        mine = offset + me
        red[mine] = sums
        copies = []
        for step in range(1, size):
            copy = pltpu.make_async_remote_copy(
                src_ref=red.at[mine],
                dst_ref=red.at[mine],
                send_sem=red_sem.at[0, sem_at],
                recv_sem=red_sem.at[1, sem_at],
                device_id=peer(step),
                device_id_type=MESH,
            )
            copy.start()
            copies.append(copy)
            sem_at += 1
        for copy in copies:
            copy.wait()
        sums = jnp.sum(red[offset : offset + size], axis=0)
        offset += size
    spot = lax.broadcasted_iota(I32, (2, TILE), 1) - system
    moment = [
        jnp.broadcast_to(
            jnp.sum(
                jnp.where(spot == 2 * q, jnp.broadcast_to(sums, (2, TILE)), 0.0),
                axis=1,
                keepdims=True,
            ),
            (2, TILE),
        )
        for q in range(moments)
    ]

    def product_of(a, b):
        total = None
        for p, a_p in enumerate(a):
            for q, b_q in enumerate(b):
                term = a_p * b_q * moment[p + q]
                total = term if total is None else total + term
        return total

    def add(a, b, factor):
        longer = max(len(a), len(b))
        out = []
        for q in range(longer):
            if q >= len(a):
                out.append(factor * b[q])
            elif q >= len(b):
                out.append(a[q])
            else:
                out.append(a[q] + factor * b[q])
        return out

    one = jnp.ones((2, TILE), F32)
    residual = [one]
    direction = [one]
    solved = []
    norm_now = moment[0]
    for iteration in range(ITERS):
        image = [middle * q for q in direction]
        image = add(image, [0.0 * one] + direction, scale)
        step_size = norm_now / product_of(direction, image)
        step_size = jnp.minimum(jnp.maximum(step_size, 1.0 / highest), 1.0 / lowest)
        solved = add(solved, direction, step_size)
        if iteration + 1 < ITERS:
            residual = add(residual, image, -step_size)
            norm_next = jnp.maximum(product_of(residual, residual), 1e-20 * moment[0])
            ratio = jnp.minimum(norm_next / norm_now, highest / lowest)
            direction = add(residual, direction, ratio)
            norm_now = norm_next
    found = vec[0]
    for factor, vector in zip(solved, basis):
        found = found + factor[None] * vector
    xs[...] = found

    for b in range(blocks):
        out_ref[:, b * TILE : (b + 1) * TILE] = xs[b]


def shards(
    sizes,
    atom_types,
    potential,
    guess,
    type_electroneg,
    type_hardness,
    local_tiles,
    local_pairs,
    local_count,
    ghost_tiles,
    ghost_blocks,
    send_rows,
):
    blocks = guess.shape[1] // TILE
    slots = local_tiles.shape[0]
    n_gx, n_gy, n_gz = sizes
    if n_gx * n_gy * n_gz <= DIRECT:
        places_held, peers = n_gx * n_gy * n_gz, n_gx * n_gy * n_gz - 1
    else:
        places_held, peers = n_gx + n_gy * n_gz, n_gx + n_gy * n_gz - 2
    vmem = pl.BlockSpec(memory_space=pltpu.VMEM)
    hbm = pl.BlockSpec(memory_space=pltpu.HBM)
    applies = ITERS + 1
    vector = (blocks, 2, TILE)
    dma = pltpu.SemaphoreType.DMA
    call = pl.pallas_call(
        functools.partial(kernel, sizes),
        out_shape=jax.ShapeDtypeStruct(guess.shape, F32),
        in_specs=[hbm] * 11,
        out_specs=vmem,
        scratch_shapes=[
            pltpu.VMEM((blocks, TILE), I32),
            pltpu.VMEM((blocks, TILE), F32),
            pltpu.VMEM(guess.shape, F32),
            pltpu.SMEM(type_electroneg.shape, F32),
            pltpu.SMEM(type_hardness.shape, F32),
            pltpu.VMEM(local_pairs.shape, I32),
            pltpu.SMEM(local_count.shape, I32),
            pltpu.VMEM(ghost_blocks.shape, I32),
            pltpu.SMEM(ghost_blocks.shape, I32),
            pltpu.VMEM(send_rows.shape, I32),
            dma((10,)),
            pltpu.VMEM((slots, TILE, TILE), jnp.bfloat16),
            pltpu.VMEM((2, blocks, TILE, TILE), jnp.bfloat16),
            pltpu.VMEM((2, blocks, TILE, TILE), jnp.bfloat16),
            pltpu.VMEM((2, blocks, TILE), I32),
            pltpu.VMEM((2, blocks, TILE), I32),
            pltpu.VMEM((blocks, TILE), I32),
            pltpu.SMEM((blocks, TILE), I32),
            pltpu.VMEM((8, TILE), I32),
            pltpu.SMEM((8, TILE), I32),
            pltpu.VMEM((blocks, TILE), I32),
            pltpu.SMEM((blocks, TILE), I32),
            pltpu.VMEM((applies,) + vector, F32),
            pltpu.VMEM((applies, 2) + vector, F32),
            pltpu.VMEM((applies, 2) + vector, F32),
            [[pltpu.VMEM(vector, F32)] * 2 for _ in range(applies)],
            pltpu.VMEM((blocks + 1, 8, TILE), F32),
            pltpu.VMEM((2, blocks, 8, TILE), F32),
            pltpu.VMEM(vector, F32),
            pltpu.VMEM(vector, F32),
            pltpu.VMEM(vector, F32),
            pltpu.VMEM(vector, F32),
            pltpu.VMEM((places_held, 1, TILE), F32),
            dma((5,)),
            dma((2, 2)),
            dma((2, applies, 2)),
            dma((2, applies, 2)),
            dma((2, peers)),
        ],
        compiler_params=pltpu.CompilerParams(
            collective_id=0, has_side_effects=True, vmem_limit_bytes=60 * 1024 * 1024
        ),
        name="charges",
    )
    return call(
        atom_types.reshape(blocks, TILE),
        potential.reshape(blocks, TILE),
        guess,
        type_electroneg,
        type_hardness,
        local_tiles,
        local_pairs,
        local_count,
        ghost_tiles,
        ghost_blocks,
        send_rows,
    )


def solution(mesh):
    everywhere = ("parts", "gx", "gy", "gz")
    in_specs = (
        P(everywhere),
        P(everywhere),
        P(None, everywhere),
        P(),
        P(),
        P(everywhere, None, None),
        P(None, everywhere),
        P(everywhere),
        P(None, everywhere, None, None),
        P(None, everywhere),
        P(None, everywhere),
    )
    sizes = tuple(mesh.shape[name] for name in ("gx", "gy", "gz"))
    return jax.shard_map(
        functools.partial(shards, sizes),
        mesh=mesh,
        in_specs=in_specs,
        out_specs=P(None, everywhere),
        check_vma=False,
    )
```

```python
import functools
import math

import jax
import jax.numpy as jnp
from jax import lax
from jax.experimental import pallas as pl
from jax.experimental.pallas import tpu as pltpu
from jax.sharding import PartitionSpec as P

TILE = 128
ITERS = 3
DIRECT = 16
REACH = 0.9
MESH = pl.DeviceIdType.MESH
F32 = jnp.float32
I32 = jnp.int32
NT = (((1,), (1,)), ((), ()))
NN = (((1,), (0,)), ((), ()))


def dot(lhs, rhs, dims):
    return lax.dot_general(lhs, rhs, dims, preferred_element_type=F32)


def places(sizes):
    n_gx, n_gy, n_gz = sizes
    across = n_gy * n_gz
    u = lax.axis_index("gx")
    v = lax.axis_index("gy") * n_gz + lax.axis_index("gz")

    def brick(u_at, v_at):
        return {"gx": u_at, "gy": v_at // n_gz, "gz": lax.rem(v_at, n_gz)}

    def shift(at, by, size):
        return lax.rem(at + by, size)

    ahead = (brick(shift(u, 1, n_gx), v), brick(u, shift(v, 1, across)))
    back = (brick(shift(u, n_gx - 1, n_gx), v), brick(u, shift(v, across - 1, across)))
    whole = n_gx * across
    if whole <= DIRECT:
        me = u * across + v

        def peer(step):
            at = lax.rem(me + step, whole)
            return brick(at // across, lax.rem(at, across))

        stages = [(whole, me, peer)]
    else:
        stages = [
            (n_gx, u, lambda step: brick(shift(u, step, n_gx), v)),
            (across, v, lambda step: brick(u, shift(v, step, across))),
        ]
    return ahead, back, stages


def kernel(
    sizes,
    types_hbm,
    potential_hbm,
    guess_hbm,
    electro_hbm,
    hard_hbm,
    local_hbm,
    pairs_hbm,
    count_hbm,
    ghost_hbm,
    gblocks_hbm,
    send_hbm,
    out_ref,
    types_ref,
    potential_ref,
    guess_ref,
    electro_ref,
    hard_ref,
    pairs_ref,
    count_ref,
    gblocks_ref,
    gblocks_s,
    send_ref,
    small_sem,
    lt,
    gt,
    gp,
    rows,
    rows_in,
    table_v,
    table_s,
    own_v,
    own_s,
    next_v,
    next_s,
    vec,
    vec_in,
    part,
    part_in,
    lh,
    gl,
    hd,
    xs,
    rs,
    ps,
    red,
    load_sem,
    rows_sem,
    vec_sem,
    part_sem,
    red_sem,
):
    blocks = types_hbm.shape[0]
    ahead, back, stages = places(sizes)

    barrier = pltpu.get_barrier_semaphore()
    greeted = 0
    for size, _, peer in stages:
        greeted += size - 1
        for step in range(1, size):
            pl.semaphore_signal(barrier, inc=1, device_id=peer(step), device_id_type=MESH)

    small = []
    for at, (source, target) in enumerate(
        (
            (send_hbm, send_ref),
            (guess_hbm, guess_ref),
            (pairs_hbm, pairs_ref),
            (count_hbm, count_ref),
            (gblocks_hbm, gblocks_ref),
            (gblocks_hbm, gblocks_s),
            (types_hbm, types_ref),
            (potential_hbm, potential_ref),
            (electro_hbm, electro_ref),
            (hard_hbm, hard_ref),
        )
    ):
        copy = pltpu.make_async_copy(source, target, small_sem.at[at])
        copy.start()
        small.append(copy)
    load_local = pltpu.make_async_copy(local_hbm, lt, load_sem.at[0])
    load_local.start()
    load_ghost = pltpu.make_async_copy(ghost_hbm, gt, load_sem.at[1])
    load_ghost.start()

    for copy in small[:2]:
        copy.wait()
    for b in range(blocks):
        cut = slice(b * TILE, (b + 1) * TILE)
        piece = send_ref[:, cut]
        rows[0, b : b + 1, :] = piece[0:1]
        rows[1, b : b + 1, :] = piece[1:2]
        begin = guess_ref[:, cut]
        vec[0, b] = begin

    pl.semaphore_wait(barrier, greeted)

    rows_copy = []
    for d in range(2):
        copy = pltpu.make_async_remote_copy(
            src_ref=rows.at[d],
            dst_ref=rows_in.at[d],
            send_sem=rows_sem.at[0, d],
            recv_sem=rows_sem.at[1, d],
            device_id=back[d],
            device_id_type=MESH,
        )
        copy.start()
        rows_copy.append(copy)

    def send(buffer, landing, sems, apply, d, target):
        copy = pltpu.make_async_remote_copy(
            src_ref=buffer,
            dst_ref=landing,
            send_sem=sems.at[0, apply, d],
            recv_sem=sems.at[1, apply, d],
            device_id=target,
            device_id_type=MESH,
        )
        copy.start()
        return copy

    first_sends = [send(vec.at[0], vec_in.at[0, d], vec_sem, 0, d, back[d]) for d in range(2)]

    for copy in small[2:]:
        copy.wait()
    slots = pairs_ref.shape[1]
    slot = lax.broadcasted_iota(I32, (blocks, slots), 1)
    block = lax.broadcasted_iota(I32, (blocks, slots), 0)
    live = slot < count_ref[0]
    pair_row = jnp.broadcast_to(pairs_ref[0:1, :], (blocks, slots))
    pair_col = jnp.broadcast_to(pairs_ref[1:2, :], (blocks, slots))
    columns = []
    partners = []
    for mine, other in ((pair_row, pair_col), (pair_col, pair_row)):
        hit = mine == block
        first = jnp.min(jnp.where(hit, slot, slots - 1), axis=1, keepdims=True)
        last = jnp.max(jnp.where(hit, slot, 0), axis=1, keepdims=True)
        for found in (first, last):
            columns.append(found)
            value = jnp.where(live, other, blocks)
            partners.append(
                jnp.max(jnp.where(slot == found, value, 0), axis=1, keepdims=True)
            )
    columns = columns + partners
    slot_g = lax.broadcasted_iota(I32, (blocks, blocks), 1)
    block_g = lax.broadcasted_iota(I32, (blocks, blocks), 0)
    for d in range(2):
        named = jnp.broadcast_to(gblocks_ref[d : d + 1, :], (blocks, blocks))
        columns.append(jnp.max(jnp.where(named == block_g, slot_g, 0), axis=1, keepdims=True))
    lane = lax.broadcasted_iota(I32, (blocks, TILE), 1)
    table = jnp.zeros((blocks, TILE), I32)
    for q, column in enumerate(columns):
        table = jnp.where(lane == q, column, table)
    table_v[...] = table
    load_table = pltpu.make_async_copy(table_v, table_s, load_sem.at[2])
    load_table.start()
    own_v[...] = jnp.zeros(own_v.shape, I32)
    slot_k = lax.broadcasted_iota(I32, (blocks, TILE), 0)
    for d in range(2):
        at = jnp.broadcast_to(rows[d][:, 0:1] // TILE, (blocks, TILE))
        own_v[d : d + 1, :] = jnp.max(
            jnp.where(at == lane, slot_k, 0), axis=0, keepdims=True
        )
    load_own = pltpu.make_async_copy(own_v, own_s, load_sem.at[3])
    load_own.start()

    types = types_ref[...]
    hard = jnp.zeros(types.shape, F32)
    electro = jnp.zeros(types.shape, F32)
    for code in range(hard_ref.shape[0]):
        hard = jnp.where(types == code, hard_ref[code], hard)
        electro = jnp.where(types == code, electro_ref[code], electro)
    wanted = -(electro + potential_ref[...])
    system = lax.broadcasted_iota(I32, (2, TILE), 0)
    least = jnp.full((2, TILE), hard_ref[0], F32)
    most = least
    for code in range(1, hard_ref.shape[0]):
        least = jnp.minimum(least, hard_ref[code])
        most = jnp.maximum(most, hard_ref[code])
    lowest = least - REACH
    highest = most + REACH
    middle = 0.5 * (least + most)
    scale = 0.5 * (most - least + REACH)
    shrink = 1.0 / scale
    for b in range(blocks):
        hd[b] = jnp.broadcast_to(hard[b : b + 1], (2, TILE))
        rs[b] = jnp.where(system == 0, jnp.broadcast_to(wanted[b : b + 1], (2, TILE)), -1.0)

    lh[blocks] = jnp.zeros((8, TILE), F32)
    top = lax.broadcasted_iota(I32, (8, TILE), 0) < 4

    def split(vector):
        upper = vector.astype(jnp.bfloat16).astype(F32)
        return jnp.concatenate([upper, vector - upper] * 2, axis=1)

    def join(one, two):
        return jnp.where(top, one, two).astype(jnp.bfloat16)

    def parts_of(both):
        one = both[0:2, :TILE] + both[2:4, :TILE]
        two = both[4:6, TILE:] + both[6:8, TILE:]
        return one, two

    def square(a, b, c, d):
        return jnp.concatenate(
            [jnp.concatenate([a, b], axis=1), jnp.concatenate([c, d], axis=1)], axis=0
        )

    def looped(steps, unroll, body):
        unroll = math.gcd(steps, unroll)

        def run(outer, carry):
            for inner in range(unroll):
                body(outer * unroll + inner)
            return carry

        lax.fori_loop(0, steps // unroll, run, 0)

    def local_part(apply, last=False):
        def body(pair):
            one = pair * 2
            two = one + 1
            s = [(table_s[one, q], table_s[two, q]) for q in range(8)]
            left = jnp.concatenate(
                [join(lh[s[4][0]], lh[s[4][1]]), join(lh[s[5][0]], lh[s[5][1]])], axis=1
            )
            onward = dot(
                left, square(lt[s[0][0]], lt[s[1][0]], lt[s[0][1]], lt[s[1][1]]), NT
            )
            if last:
                sum_one, sum_two = parts_of(onward)
                ps[one] = hd[one] * vec[apply, one] + 2.0 * sum_one
                ps[two] = hd[two] * vec[apply, two] + 2.0 * sum_two
                return
            left = jnp.concatenate(
                [join(lh[s[6][0]], lh[s[6][1]]), join(lh[s[7][0]], lh[s[7][1]])], axis=1
            )
            behind = dot(
                left, square(lt[s[2][0]], lt[s[2][1]], lt[s[3][0]], lt[s[3][1]]), NN
            )
            sum_one, sum_two = parts_of(onward + behind)
            ps[one] = hd[one] * vec[apply, one] + sum_one
            ps[two] = hd[two] * vec[apply, two] + sum_two

        looped(blocks // 2, 16, body)

    def partials(apply):
        def body(k):
            left = join(lh[gblocks_s[0, k]], lh[gblocks_s[1, k]])
            both = dot(left, jnp.concatenate([gp[0, k], gp[1, k]], axis=1), NN)
            zero, first = parts_of(both)
            part[apply, 0, k] = zero
            part[apply, 1, k] = first

        looped(blocks, 32, body)

    def ghost_part(last):
        def body(pair):
            one = pair * 2
            two = one + 1
            k0 = (table_s[one, 8], table_s[two, 8])
            k1 = (table_s[one, 9], table_s[two, 9])
            left = jnp.concatenate(
                [
                    join(gl[0, next_s[k0[0], 0]], gl[0, next_s[k0[1], 0]]),
                    join(gl[1, next_s[k1[0], 1]], gl[1, next_s[k1[1], 1]]),
                ],
                axis=1,
            )
            sum_one, sum_two = parts_of(
                dot(left, square(gp[0, k0[0]], gp[1, k1[0]], gp[0, k0[1]], gp[1, k1[1]]), NT)
            )
            if last:
                sum_one, sum_two = 2.0 * sum_one, 2.0 * sum_two
            ps[one] = ps[one] + sum_one
            ps[two] = ps[two] + sum_two

        looped(blocks // 2, 16, body)

    def returned(apply):
        def body(b):
            ps[b] = ps[b] + (part_in[apply][0][own_s[0, b]] + part_in[apply][1][own_s[1, b]])

        looped(blocks, 32, body)

    def reorder():
        within_at = lax.broadcasted_iota(I32, (TILE, TILE), 0)

        for d in range(2):

            def body(k):
                within = rows_in[d, pl.ds(k, 1), :]
                within = within - (within // TILE) * TILE
                chosen = jnp.where(within == within_at, 1.0, 0.0).astype(jnp.bfloat16)
                gp[d, k] = dot(gt[d, k], chosen, NT).astype(jnp.bfloat16)

            looped(blocks, 16, body)

    for apply in range(ITERS + 1):
        last = apply == ITERS
        if apply == 0:
            incoming = first_sends
        else:
            incoming = [
                send(vec.at[apply], vec_in.at[apply, d], vec_sem, apply, d, back[d])
                for d in range(2)
            ]
        lh[0:blocks] = split(vec[apply])
        if apply == 0:
            load_local.wait()
            load_table.wait()
            local_part(apply)
            load_ghost.wait()
            for copy in rows_copy:
                copy.wait()
            columns = jnp.zeros((blocks, TILE), I32)
            for d in range(2):
                columns = jnp.where(lane == d, rows_in[d][:, 0:1] // TILE, columns)
            next_v[...] = columns
            load_next = pltpu.make_async_copy(next_v, next_s, load_sem.at[4])
            load_next.start()
            reorder()
            load_next.wait()
            load_own.wait()
        back_copies = []
        if not last:
            partials(apply)
            for d in range(2):
                back_copies.append(
                    send(part.at[apply, d], part_in[apply][d], part_sem, apply, d, ahead[d])
                )
        if apply > 0:
            local_part(apply, last)
        for d in range(2):
            incoming[d].wait()
            gl[d] = split(vec_in[apply, d])
        ghost_part(last)
        for copy in back_copies:
            copy.wait()
        if not last:
            returned(apply)
        product = ps[...]
        if apply == 0:
            vec[1] = rs[...] - product
        elif apply < ITERS:
            vec[apply + 1] = (product - middle[None] * vec[apply]) * shrink[None]
        else:
            beyond = (product - middle[None] * vec[apply]) * shrink[None]

    basis = [vec[apply] for apply in range(1, ITERS + 1)] + [beyond]
    moments = 2 * ITERS
    dots = [jnp.sum(basis[q // 2] * basis[(q + 1) // 2], axis=0) for q in range(moments)]
    dots += [jnp.zeros((2, TILE), F32)] * (-moments % 4)
    dots = jnp.concatenate(dots, axis=0)
    sums = jnp.sum(dots, axis=1, keepdims=True)
    lanes = lax.broadcasted_iota(I32, dots.shape, 1)
    lines = lax.broadcasted_iota(I32, dots.shape, 0)
    sums = jnp.sum(
        jnp.where(lanes == lines, jnp.broadcast_to(sums, dots.shape), 0.0), axis=0, keepdims=True
    )
    offset = 0
    sem_at = 0
    for size, me, peer in stages:
        mine = offset + me
        red[mine] = sums
        copies = []
        for step in range(1, size):
            copy = pltpu.make_async_remote_copy(
                src_ref=red.at[mine],
                dst_ref=red.at[mine],
                send_sem=red_sem.at[0, sem_at],
                recv_sem=red_sem.at[1, sem_at],
                device_id=peer(step),
                device_id_type=MESH,
            )
            copy.start()
            copies.append(copy)
            sem_at += 1
        for copy in copies:
            copy.wait()
        sums = jnp.sum(red[offset : offset + size], axis=0)
        offset += size
    spot = lax.broadcasted_iota(I32, (2, TILE), 1) - system
    moment = [
        jnp.broadcast_to(
            jnp.sum(
                jnp.where(spot == 2 * q, jnp.broadcast_to(sums, (2, TILE)), 0.0),
                axis=1,
                keepdims=True,
            ),
            (2, TILE),
        )
        for q in range(moments)
    ]

    def product_of(a, b):
        total = None
        for p, a_p in enumerate(a):
            for q, b_q in enumerate(b):
                term = a_p * b_q * moment[p + q]
                total = term if total is None else total + term
        return total

    def add(a, b, factor):
        longer = max(len(a), len(b))
        out = []
        for q in range(longer):
            if q >= len(a):
                out.append(factor * b[q])
            elif q >= len(b):
                out.append(a[q])
            else:
                out.append(a[q] + factor * b[q])
        return out

    one = jnp.ones((2, TILE), F32)
    residual = [one]
    direction = [one]
    solved = []
    norm_now = moment[0]
    for iteration in range(ITERS):
        image = [middle * q for q in direction]
        image = add(image, [0.0 * one] + direction, scale)
        step_size = norm_now / product_of(direction, image)
        step_size = jnp.minimum(jnp.maximum(step_size, 1.0 / highest), 1.0 / lowest)
        solved = add(solved, direction, step_size)
        if iteration + 1 < ITERS:
            residual = add(residual, image, -step_size)
            norm_next = jnp.maximum(product_of(residual, residual), 1e-20 * moment[0])
            ratio = jnp.minimum(norm_next / norm_now, highest / lowest)
            direction = add(residual, direction, ratio)
            norm_now = norm_next
    found = vec[0]
    for factor, vector in zip(solved, basis):
        found = found + factor[None] * vector
    xs[...] = found

    for b in range(blocks):
        out_ref[:, b * TILE : (b + 1) * TILE] = xs[b]


def shards(
    sizes,
    atom_types,
    potential,
    guess,
    type_electroneg,
    type_hardness,
    local_tiles,
    local_pairs,
    local_count,
    ghost_tiles,
    ghost_blocks,
    send_rows,
):
    blocks = guess.shape[1] // TILE
    slots = local_tiles.shape[0]
    n_gx, n_gy, n_gz = sizes
    if n_gx * n_gy * n_gz <= DIRECT:
        places_held, peers = n_gx * n_gy * n_gz, n_gx * n_gy * n_gz - 1
    else:
        places_held, peers = n_gx + n_gy * n_gz, n_gx + n_gy * n_gz - 2
    vmem = pl.BlockSpec(memory_space=pltpu.VMEM)
    hbm = pl.BlockSpec(memory_space=pltpu.HBM)
    applies = ITERS + 1
    vector = (blocks, 2, TILE)
    dma = pltpu.SemaphoreType.DMA
    call = pl.pallas_call(
        functools.partial(kernel, sizes),
        out_shape=jax.ShapeDtypeStruct(guess.shape, F32),
        in_specs=[hbm] * 11,
        out_specs=vmem,
        scratch_shapes=[
            pltpu.VMEM((blocks, TILE), I32),
            pltpu.VMEM((blocks, TILE), F32),
            pltpu.VMEM(guess.shape, F32),
            pltpu.SMEM(type_electroneg.shape, F32),
            pltpu.SMEM(type_hardness.shape, F32),
            pltpu.VMEM(local_pairs.shape, I32),
            pltpu.SMEM(local_count.shape, I32),
            pltpu.VMEM(ghost_blocks.shape, I32),
            pltpu.SMEM(ghost_blocks.shape, I32),
            pltpu.VMEM(send_rows.shape, I32),
            dma((10,)),
            pltpu.VMEM((slots, TILE, TILE), jnp.bfloat16),
            pltpu.VMEM((2, blocks, TILE, TILE), jnp.bfloat16),
            pltpu.VMEM((2, blocks, TILE, TILE), jnp.bfloat16),
            pltpu.VMEM((2, blocks, TILE), I32),
            pltpu.VMEM((2, blocks, TILE), I32),
            pltpu.VMEM((blocks, TILE), I32),
            pltpu.SMEM((blocks, TILE), I32),
            pltpu.VMEM((8, TILE), I32),
            pltpu.SMEM((8, TILE), I32),
            pltpu.VMEM((blocks, TILE), I32),
            pltpu.SMEM((blocks, TILE), I32),
            pltpu.VMEM((applies,) + vector, F32),
            pltpu.VMEM((applies, 2) + vector, F32),
            pltpu.VMEM((applies, 2) + vector, F32),
            [[pltpu.VMEM(vector, F32)] * 2 for _ in range(applies)],
            pltpu.VMEM((blocks + 1, 8, TILE), F32),
            pltpu.VMEM((2, blocks, 8, TILE), F32),
            pltpu.VMEM(vector, F32),
            pltpu.VMEM(vector, F32),
            pltpu.VMEM(vector, F32),
            pltpu.VMEM(vector, F32),
            pltpu.VMEM((places_held, 1, TILE), F32),
            dma((5,)),
            dma((2, 2)),
            dma((2, applies, 2)),
            dma((2, applies, 2)),
            dma((2, peers)),
        ],
        compiler_params=pltpu.CompilerParams(
            collective_id=0, has_side_effects=True, vmem_limit_bytes=60 * 1024 * 1024
        ),
        name="charges",
    )
    return call(
        atom_types.reshape(blocks, TILE),
        potential.reshape(blocks, TILE),
        guess,
        type_electroneg,
        type_hardness,
        local_tiles,
        local_pairs,
        local_count,
        ghost_tiles,
        ghost_blocks,
        send_rows,
    )


def solution(mesh):
    everywhere = ("parts", "gx", "gy", "gz")
    in_specs = (
        P(everywhere),
        P(everywhere),
        P(None, everywhere),
        P(),
        P(),
        P(everywhere, None, None),
        P(None, everywhere),
        P(everywhere),
        P(None, everywhere, None, None),
        P(None, everywhere),
        P(None, everywhere),
    )
    sizes = tuple(mesh.shape[name] for name in ("gx", "gy", "gz"))
    return jax.shard_map(
        functools.partial(shards, sizes),
        mesh=mesh,
        in_specs=in_specs,
        out_specs=P(None, everywhere),
        check_vma=False,
    )
```

```python
import functools
import math

import jax
import jax.numpy as jnp
from jax import lax
from jax.experimental import pallas as pl
from jax.experimental.pallas import tpu as pltpu
from jax.sharding import PartitionSpec as P

TILE = 128
ITERS = 3
DIRECT = 16
REACH = 0.9
MESH = pl.DeviceIdType.MESH
F32 = jnp.float32
I32 = jnp.int32
NT = (((1,), (1,)), ((), ()))
NN = (((1,), (0,)), ((), ()))


def dot(lhs, rhs, dims):
    return lax.dot_general(lhs, rhs, dims, preferred_element_type=F32)


def places(sizes):
    n_gx, n_gy, n_gz = sizes
    across = n_gy * n_gz
    u = lax.axis_index("gx")
    v = lax.axis_index("gy") * n_gz + lax.axis_index("gz")

    def brick(u_at, v_at):
        return {"gx": u_at, "gy": v_at // n_gz, "gz": lax.rem(v_at, n_gz)}

    def shift(at, by, size):
        return lax.rem(at + by, size)

    ahead = (brick(shift(u, 1, n_gx), v), brick(u, shift(v, 1, across)))
    back = (brick(shift(u, n_gx - 1, n_gx), v), brick(u, shift(v, across - 1, across)))
    whole = n_gx * across
    if whole <= DIRECT:
        me = u * across + v

        def peer(step):
            at = lax.rem(me + step, whole)
            return brick(at // across, lax.rem(at, across))

        stages = [(whole, me, peer)]
    else:
        stages = [
            (n_gx, u, lambda step: brick(shift(u, step, n_gx), v)),
            (across, v, lambda step: brick(u, shift(v, step, across))),
        ]
    return ahead, back, stages


def kernel(
    sizes,
    types_hbm,
    potential_hbm,
    guess_hbm,
    electro_hbm,
    hard_hbm,
    local_hbm,
    pairs_hbm,
    count_hbm,
    ghost_hbm,
    gblocks_hbm,
    send_hbm,
    out_ref,
    types_ref,
    potential_ref,
    guess_ref,
    electro_ref,
    hard_ref,
    pairs_ref,
    count_ref,
    gblocks_ref,
    gblocks_s,
    send_ref,
    small_sem,
    lt,
    gt,
    gp,
    rows,
    rows_in,
    table_v,
    table_s,
    own_v,
    own_s,
    next_v,
    next_s,
    vec,
    vec_in,
    part,
    part_in,
    lh,
    gl,
    hd,
    xs,
    rs,
    ps,
    red,
    load_sem,
    rows_sem,
    vec_sem,
    part_sem,
    red_sem,
):
    blocks = types_hbm.shape[0]
    ahead, back, stages = places(sizes)

    barrier = pltpu.get_barrier_semaphore()
    greeted = 0
    for size, _, peer in stages:
        greeted += size - 1
        for step in range(1, size):
            pl.semaphore_signal(barrier, inc=1, device_id=peer(step), device_id_type=MESH)

    small = []
    for at, (source, target) in enumerate(
        (
            (send_hbm, send_ref),
            (guess_hbm, guess_ref),
            (pairs_hbm, pairs_ref),
            (count_hbm, count_ref),
            (gblocks_hbm, gblocks_ref),
            (gblocks_hbm, gblocks_s),
            (types_hbm, types_ref),
            (potential_hbm, potential_ref),
            (electro_hbm, electro_ref),
            (hard_hbm, hard_ref),
        )
    ):
        copy = pltpu.make_async_copy(source, target, small_sem.at[at])
        copy.start()
        small.append(copy)
    load_local = pltpu.make_async_copy(local_hbm, lt, load_sem.at[0])
    load_local.start()
    load_ghost = pltpu.make_async_copy(ghost_hbm, gt, load_sem.at[1])
    load_ghost.start()

    for copy in small[:2]:
        copy.wait()
    for b in range(blocks):
        cut = slice(b * TILE, (b + 1) * TILE)
        piece = send_ref[:, cut]
        rows[0, b : b + 1, :] = piece[0:1]
        rows[1, b : b + 1, :] = piece[1:2]
        begin = guess_ref[:, cut]
        vec[0, b] = begin

    pl.semaphore_wait(barrier, greeted)

    rows_copy = []
    for d in range(2):
        copy = pltpu.make_async_remote_copy(
            src_ref=rows.at[d],
            dst_ref=rows_in.at[d],
            send_sem=rows_sem.at[0, d],
            recv_sem=rows_sem.at[1, d],
            device_id=back[d],
            device_id_type=MESH,
        )
        copy.start()
        rows_copy.append(copy)

    def send(buffer, landing, sems, apply, d, target):
        copy = pltpu.make_async_remote_copy(
            src_ref=buffer,
            dst_ref=landing,
            send_sem=sems.at[0, apply, d],
            recv_sem=sems.at[1, apply, d],
            device_id=target,
            device_id_type=MESH,
        )
        copy.start()
        return copy

    first_sends = [send(vec.at[0], vec_in.at[0, d], vec_sem, 0, d, back[d]) for d in range(2)]

    for copy in small[2:]:
        copy.wait()
    slots = pairs_ref.shape[1]
    slot = lax.broadcasted_iota(I32, (blocks, slots), 1)
    block = lax.broadcasted_iota(I32, (blocks, slots), 0)
    live = slot < count_ref[0]
    pair_row = jnp.broadcast_to(pairs_ref[0:1, :], (blocks, slots))
    pair_col = jnp.broadcast_to(pairs_ref[1:2, :], (blocks, slots))
    columns = []
    partners = []
    for mine, other in ((pair_row, pair_col), (pair_col, pair_row)):
        hit = mine == block
        first = jnp.min(jnp.where(hit, slot, slots - 1), axis=1, keepdims=True)
        last = jnp.max(jnp.where(hit, slot, 0), axis=1, keepdims=True)
        for found in (first, last):
            columns.append(found)
            value = jnp.where(live, other, blocks)
            partners.append(
                jnp.max(jnp.where(slot == found, value, 0), axis=1, keepdims=True)
            )
    columns = columns + partners
    slot_g = lax.broadcasted_iota(I32, (blocks, blocks), 1)
    block_g = lax.broadcasted_iota(I32, (blocks, blocks), 0)
    for d in range(2):
        named = jnp.broadcast_to(gblocks_ref[d : d + 1, :], (blocks, blocks))
        columns.append(jnp.max(jnp.where(named == block_g, slot_g, 0), axis=1, keepdims=True))
    lane = lax.broadcasted_iota(I32, (blocks, TILE), 1)
    table = jnp.zeros((blocks, TILE), I32)
    for q, column in enumerate(columns):
        table = jnp.where(lane == q, column, table)
    table_v[...] = table
    load_table = pltpu.make_async_copy(table_v, table_s, load_sem.at[2])
    load_table.start()
    own_v[...] = jnp.zeros(own_v.shape, I32)
    slot_k = lax.broadcasted_iota(I32, (blocks, TILE), 0)
    for d in range(2):
        at = jnp.broadcast_to(rows[d][:, 0:1] // TILE, (blocks, TILE))
        own_v[d : d + 1, :] = jnp.max(
            jnp.where(at == lane, slot_k, 0), axis=0, keepdims=True
        )
    load_own = pltpu.make_async_copy(own_v, own_s, load_sem.at[3])
    load_own.start()

    types = types_ref[...]
    hard = jnp.zeros(types.shape, F32)
    electro = jnp.zeros(types.shape, F32)
    for code in range(hard_ref.shape[0]):
        hard = jnp.where(types == code, hard_ref[code], hard)
        electro = jnp.where(types == code, electro_ref[code], electro)
    wanted = -(electro + potential_ref[...])
    system = lax.broadcasted_iota(I32, (2, TILE), 0)
    least = jnp.full((2, TILE), hard_ref[0], F32)
    most = least
    for code in range(1, hard_ref.shape[0]):
        least = jnp.minimum(least, hard_ref[code])
        most = jnp.maximum(most, hard_ref[code])
    lowest = least - REACH
    highest = most + REACH
    middle = 0.5 * (least + most)
    scale = 0.5 * (most - least + REACH)
    shrink = 1.0 / scale
    for b in range(blocks):
        hd[b] = jnp.broadcast_to(hard[b : b + 1], (2, TILE))
        rs[b] = jnp.where(system == 0, jnp.broadcast_to(wanted[b : b + 1], (2, TILE)), -1.0)

    lh[blocks] = jnp.zeros((8, TILE), F32)
    top = lax.broadcasted_iota(I32, (8, TILE), 0) < 4

    def split(vector):
        upper = vector.astype(jnp.bfloat16).astype(F32)
        return jnp.concatenate([upper, vector - upper] * 2, axis=1)

    def join(one, two):
        return jnp.where(top, one, two).astype(jnp.bfloat16)

    def parts_of(both):
        one = both[0:2, :TILE] + both[2:4, :TILE]
        two = both[4:6, TILE:] + both[6:8, TILE:]
        return one, two

    def square(a, b, c, d):
        return jnp.concatenate(
            [jnp.concatenate([a, b], axis=1), jnp.concatenate([c, d], axis=1)], axis=0
        )

    def looped(steps, unroll, body):
        unroll = math.gcd(steps, unroll)

        def run(outer, carry):
            for inner in range(unroll):
                body(outer * unroll + inner)
            return carry

        lax.fori_loop(0, steps // unroll, run, 0)

    def local_part(apply, last=False):
        def body(pair):
            one = pair * 2
            two = one + 1
            s = [(table_s[one, q], table_s[two, q]) for q in range(8)]
            left = jnp.concatenate(
                [join(lh[s[4][0]], lh[s[4][1]]), join(lh[s[5][0]], lh[s[5][1]])], axis=1
            )
            onward = dot(
                left, square(lt[s[0][0]], lt[s[1][0]], lt[s[0][1]], lt[s[1][1]]), NT
            )
            if last:
                sum_one, sum_two = parts_of(onward)
                ps[one] = hd[one] * vec[apply, one] + 2.0 * sum_one
                ps[two] = hd[two] * vec[apply, two] + 2.0 * sum_two
                return
            left = jnp.concatenate(
                [join(lh[s[6][0]], lh[s[6][1]]), join(lh[s[7][0]], lh[s[7][1]])], axis=1
            )
            behind = dot(
                left, square(lt[s[2][0]], lt[s[2][1]], lt[s[3][0]], lt[s[3][1]]), NN
            )
            sum_one, sum_two = parts_of(onward + behind)
            ps[one] = hd[one] * vec[apply, one] + sum_one
            ps[two] = hd[two] * vec[apply, two] + sum_two

        looped(blocks // 2, 16, body)

    def partials(apply):
        def body(k):
            left = join(lh[gblocks_s[0, k]], lh[gblocks_s[1, k]])
            both = dot(left, jnp.concatenate([gp[0, k], gp[1, k]], axis=1), NN)
            zero, first = parts_of(both)
            part[apply, 0, k] = zero
            part[apply, 1, k] = first

        looped(blocks, 32, body)

    def ghost_part(last):
        def body(pair):
            one = pair * 2
            two = one + 1
            k0 = (table_s[one, 8], table_s[two, 8])
            k1 = (table_s[one, 9], table_s[two, 9])
            left = jnp.concatenate(
                [
                    join(gl[0, next_s[k0[0], 0]], gl[0, next_s[k0[1], 0]]),
                    join(gl[1, next_s[k1[0], 1]], gl[1, next_s[k1[1], 1]]),
                ],
                axis=1,
            )
            sum_one, sum_two = parts_of(
                dot(left, square(gp[0, k0[0]], gp[1, k1[0]], gp[0, k0[1]], gp[1, k1[1]]), NT)
            )
            if last:
                sum_one, sum_two = 2.0 * sum_one, 2.0 * sum_two
            ps[one] = ps[one] + sum_one
            ps[two] = ps[two] + sum_two

        looped(blocks // 2, 16, body)

    def returned(apply):
        def body(b):
            ps[b] = ps[b] + (part_in[apply][0][own_s[0, b]] + part_in[apply][1][own_s[1, b]])

        looped(blocks, 32, body)

    def reorder():
        within_at = lax.broadcasted_iota(I32, (TILE, TILE), 0)

        for d in range(2):

            def body(k):
                within = rows_in[d, pl.ds(k, 1), :]
                within = within - (within // TILE) * TILE
                chosen = jnp.where(within == within_at, 1.0, 0.0).astype(jnp.bfloat16)
                gp[d, k] = dot(gt[d, k], chosen, NT).astype(jnp.bfloat16)

            looped(blocks, 16, body)

    for apply in range(ITERS + 1):
        last = apply == ITERS
        if apply == 0:
            incoming = first_sends
        else:
            incoming = [
                send(vec.at[apply], vec_in.at[apply, d], vec_sem, apply, d, back[d])
                for d in range(2)
            ]
        lh[0:blocks] = split(vec[apply])
        if apply == 0:
            load_local.wait()
            load_table.wait()
            local_part(apply)
            load_ghost.wait()
            for copy in rows_copy:
                copy.wait()
            columns = jnp.zeros((blocks, TILE), I32)
            for d in range(2):
                columns = jnp.where(lane == d, rows_in[d][:, 0:1] // TILE, columns)
            next_v[...] = columns
            load_next = pltpu.make_async_copy(next_v, next_s, load_sem.at[4])
            load_next.start()
            reorder()
            load_next.wait()
            load_own.wait()
        back_copies = []
        if not last:
            partials(apply)
            for d in range(2):
                back_copies.append(
                    send(part.at[apply, d], part_in[apply][d], part_sem, apply, d, ahead[d])
                )
        if apply > 0:
            local_part(apply, last)
        if last:
            early = [
                jnp.sum(vec[1 + q // 2] * vec[1 + (q + 1) // 2], axis=0)
                for q in range(2 * ITERS - 1)
            ]
        for d in range(2):
            incoming[d].wait()
            gl[d] = split(vec_in[apply, d])
        ghost_part(last)
        for copy in back_copies:
            copy.wait()
        if not last:
            returned(apply)
        product = ps[...]
        if apply == 0:
            vec[1] = rs[...] - product
        elif apply < ITERS:
            vec[apply + 1] = (product - middle[None] * vec[apply]) * shrink[None]
        else:
            beyond = (product - middle[None] * vec[apply]) * shrink[None]

    basis = [vec[apply] for apply in range(1, ITERS + 1)] + [beyond]
    moments = 2 * ITERS
    dots = early + [jnp.sum(basis[ITERS - 1] * beyond, axis=0)]
    dots += [jnp.zeros((2, TILE), F32)] * (-moments % 4)
    dots = jnp.concatenate(dots, axis=0)
    sums = jnp.sum(dots, axis=1, keepdims=True)
    lanes = lax.broadcasted_iota(I32, dots.shape, 1)
    lines = lax.broadcasted_iota(I32, dots.shape, 0)
    sums = jnp.sum(
        jnp.where(lanes == lines, jnp.broadcast_to(sums, dots.shape), 0.0), axis=0, keepdims=True
    )
    offset = 0
    sem_at = 0
    for size, me, peer in stages:
        mine = offset + me
        red[mine] = sums
        copies = []
        for step in range(1, size):
            copy = pltpu.make_async_remote_copy(
                src_ref=red.at[mine],
                dst_ref=red.at[mine],
                send_sem=red_sem.at[0, sem_at],
                recv_sem=red_sem.at[1, sem_at],
                device_id=peer(step),
                device_id_type=MESH,
            )
            copy.start()
            copies.append(copy)
            sem_at += 1
        for copy in copies:
            copy.wait()
        sums = jnp.sum(red[offset : offset + size], axis=0)
        offset += size
    spot = lax.broadcasted_iota(I32, (2, TILE), 1) - system
    moment = [
        jnp.broadcast_to(
            jnp.sum(
                jnp.where(spot == 2 * q, jnp.broadcast_to(sums, (2, TILE)), 0.0),
                axis=1,
                keepdims=True,
            ),
            (2, TILE),
        )
        for q in range(moments)
    ]

    def product_of(a, b):
        total = None
        for p, a_p in enumerate(a):
            for q, b_q in enumerate(b):
                term = a_p * b_q * moment[p + q]
                total = term if total is None else total + term
        return total

    def add(a, b, factor):
        longer = max(len(a), len(b))
        out = []
        for q in range(longer):
            if q >= len(a):
                out.append(factor * b[q])
            elif q >= len(b):
                out.append(a[q])
            else:
                out.append(a[q] + factor * b[q])
        return out

    one = jnp.ones((2, TILE), F32)
    residual = [one]
    direction = [one]
    solved = []
    norm_now = moment[0]
    for iteration in range(ITERS):
        image = [middle * q for q in direction]
        image = add(image, [0.0 * one] + direction, scale)
        step_size = norm_now / product_of(direction, image)
        step_size = jnp.minimum(jnp.maximum(step_size, 1.0 / highest), 1.0 / lowest)
        solved = add(solved, direction, step_size)
        if iteration + 1 < ITERS:
            residual = add(residual, image, -step_size)
            norm_next = jnp.maximum(product_of(residual, residual), 1e-20 * moment[0])
            ratio = jnp.minimum(norm_next / norm_now, highest / lowest)
            direction = add(residual, direction, ratio)
            norm_now = norm_next
    found = vec[0]
    for factor, vector in zip(solved, basis):
        found = found + factor[None] * vector
    xs[...] = found

    for b in range(blocks):
        out_ref[:, b * TILE : (b + 1) * TILE] = xs[b]


def shards(
    sizes,
    atom_types,
    potential,
    guess,
    type_electroneg,
    type_hardness,
    local_tiles,
    local_pairs,
    local_count,
    ghost_tiles,
    ghost_blocks,
    send_rows,
):
    blocks = guess.shape[1] // TILE
    slots = local_tiles.shape[0]
    n_gx, n_gy, n_gz = sizes
    if n_gx * n_gy * n_gz <= DIRECT:
        places_held, peers = n_gx * n_gy * n_gz, n_gx * n_gy * n_gz - 1
    else:
        places_held, peers = n_gx + n_gy * n_gz, n_gx + n_gy * n_gz - 2
    vmem = pl.BlockSpec(memory_space=pltpu.VMEM)
    hbm = pl.BlockSpec(memory_space=pltpu.HBM)
    applies = ITERS + 1
    vector = (blocks, 2, TILE)
    dma = pltpu.SemaphoreType.DMA
    call = pl.pallas_call(
        functools.partial(kernel, sizes),
        out_shape=jax.ShapeDtypeStruct(guess.shape, F32),
        in_specs=[hbm] * 11,
        out_specs=vmem,
        scratch_shapes=[
            pltpu.VMEM((blocks, TILE), I32),
            pltpu.VMEM((blocks, TILE), F32),
            pltpu.VMEM(guess.shape, F32),
            pltpu.SMEM(type_electroneg.shape, F32),
            pltpu.SMEM(type_hardness.shape, F32),
            pltpu.VMEM(local_pairs.shape, I32),
            pltpu.SMEM(local_count.shape, I32),
            pltpu.VMEM(ghost_blocks.shape, I32),
            pltpu.SMEM(ghost_blocks.shape, I32),
            pltpu.VMEM(send_rows.shape, I32),
            dma((10,)),
            pltpu.VMEM((slots, TILE, TILE), jnp.bfloat16),
            pltpu.VMEM((2, blocks, TILE, TILE), jnp.bfloat16),
            pltpu.VMEM((2, blocks, TILE, TILE), jnp.bfloat16),
            pltpu.VMEM((2, blocks, TILE), I32),
            pltpu.VMEM((2, blocks, TILE), I32),
            pltpu.VMEM((blocks, TILE), I32),
            pltpu.SMEM((blocks, TILE), I32),
            pltpu.VMEM((8, TILE), I32),
            pltpu.SMEM((8, TILE), I32),
            pltpu.VMEM((blocks, TILE), I32),
            pltpu.SMEM((blocks, TILE), I32),
            pltpu.VMEM((applies,) + vector, F32),
            pltpu.VMEM((applies, 2) + vector, F32),
            pltpu.VMEM((applies, 2) + vector, F32),
            [[pltpu.VMEM(vector, F32)] * 2 for _ in range(applies)],
            pltpu.VMEM((blocks + 1, 8, TILE), F32),
            pltpu.VMEM((2, blocks, 8, TILE), F32),
            pltpu.VMEM(vector, F32),
            pltpu.VMEM(vector, F32),
            pltpu.VMEM(vector, F32),
            pltpu.VMEM(vector, F32),
            pltpu.VMEM((places_held, 1, TILE), F32),
            dma((5,)),
            dma((2, 2)),
            dma((2, applies, 2)),
            dma((2, applies, 2)),
            dma((2, peers)),
        ],
        compiler_params=pltpu.CompilerParams(
            collective_id=0, has_side_effects=True, vmem_limit_bytes=60 * 1024 * 1024
        ),
        name="charges",
    )
    return call(
        atom_types.reshape(blocks, TILE),
        potential.reshape(blocks, TILE),
        guess,
        type_electroneg,
        type_hardness,
        local_tiles,
        local_pairs,
        local_count,
        ghost_tiles,
        ghost_blocks,
        send_rows,
    )


def solution(mesh):
    everywhere = ("parts", "gx", "gy", "gz")
    in_specs = (
        P(everywhere),
        P(everywhere),
        P(None, everywhere),
        P(),
        P(),
        P(everywhere, None, None),
        P(None, everywhere),
        P(everywhere),
        P(None, everywhere, None, None),
        P(None, everywhere),
        P(None, everywhere),
    )
    sizes = tuple(mesh.shape[name] for name in ("gx", "gy", "gz"))
    return jax.shard_map(
        functools.partial(shards, sizes),
        mesh=mesh,
        in_specs=in_specs,
        out_specs=P(None, everywhere),
        check_vma=False,
    )
```
